256 devices in a mesh: dp: 4 (over y), group: 16 (over z, core), tensor: 4 (over x).
Axes of the slice: x: 4, y: 4, z: 8, core: 2. Of those that a mesh axis runs over, the one named last changes fastest.
Arguments:
- queries: bfloat16 [4, 16, 512, 2560], P('dp', 'group', None, 'tensor'), may hold values from -60 to 60
- comp_kv: bfloat16 [4, 16, 512, 2, 512], P('dp', 'group', None, None, 'tensor'), may hold values from -6 to 6
- prompt_kv: bfloat16 [4, 4096, 2, 512], P('dp', 'group', None, 'tensor'), may hold values from -6 to 6
- residual: bfloat16 [4, 16, 512, 5120], P('dp', 'group', 'tensor'), may hold values from -1.796875 to 1.796875
- out_weight: bfloat16 [2560, 5120], P('tensor', ('dp', 'group')), may hold values from -0.125 to 0.125
- gain: float32 [5120], replicated, may hold values from 0.1 to 1.9
- lengths: int32 [4, 16], P('dp', 'group'), may hold values from 128 to 512, as said below
Outputs:
- attended: bfloat16 [4, 16, 512, 5120], P('dp', 'group', 'tensor')
- normed: bfloat16 [4, 16, 512, 5120], P('dp', 'group', 'tensor')
The draws below stay inside these ranges and needn't reach their ends.
Inputs may be any that keep to these rules, and one draw needn't show every extreme that they name: `lengths`: each completion has between a quarter of 512 and 512 live tokens, and some completion has 512.
All inputs are finite; a program needn't handle non-finite values.
Results may differ from the reference program's by a relative error of at most 0.015.
Values may be sent and summed in bfloat16 or wider, within the bound.
No kernel may reach another device: no remote copies, remote signals or barrier semaphores. Data moves between devices by JAX's collectives and lax.ppermute only.
A program may use at most 128 MiB of HBM per device.

```python
import jax
import jax.numpy as jnp
from jax import lax

D = 5120
QH = 20
KVH = 4
HD = 128
PLEN = 4096
CLEN = 512
PROMPTS = 4
COMPS = 16
N_TENSOR = 4


def prompt_base(key):
    inner = jax.random.fold_in(key, 101)
    shape = (PROMPTS, PLEN, 2, KVH * HD)
    bell = jax.random.truncated_normal(jax.random.fold_in(inner, 2), -6.0, 6.0, shape, jnp.float32)
    return bell


def draw_prompt_kv(key, part):
    pairs = prompt_base(key)
    return pairs.astype(jnp.bfloat16)


def draw_queries(key, part):
    shape = (PROMPTS, COMPS, CLEN, QH * HD)
    key = jax.random.fold_in(key, 3)
    return (2.5 * jax.random.truncated_normal(key, -6.0, 6.0, shape, jnp.float32)).astype(jnp.bfloat16)


def draw_comp_kv(key, part):
    key = jax.random.fold_in(key, 5)
    shape = (PROMPTS, COMPS, CLEN, 2, KVH * HD)
    return jax.random.truncated_normal(key, -6.0, 6.0, shape, jnp.float32).astype(jnp.bfloat16)


def draw_lengths(key, part):
    key = jax.random.fold_in(key, 7)
    counts = jax.random.randint(jax.random.fold_in(key, 1), (PROMPTS * COMPS,), CLEN // 4, CLEN + 1)
    fullest = jax.random.randint(jax.random.fold_in(key, 2), (), 0, PROMPTS * COMPS)
    counts = counts.at[fullest].set(CLEN)
    return counts.reshape(PROMPTS, COMPS).astype(jnp.int32)


def block_scale(key, extent, cuts, smallest, largest):
    def one(position, shards_of):
        heights = jax.random.uniform(jax.random.fold_in(jax.random.fold_in(key, 6), position), (shards_of,), jnp.float32, smallest / len(cuts), largest / len(cuts))
        return jnp.repeat(jnp.exp(heights), extent[position] // shards_of).reshape((-1,) + (1,) * (len(extent) - position - 1))

    level = one(*cuts[0])
    for cut in cuts[1:]:
        level = level * one(*cut)
    return level


def scatter_about(stream_key, dims, width, most, pieces=(), held_as=jnp.bfloat16):
    entries = width * jax.random.normal(stream_key, dims, jnp.float32)
    if pieces:
        entries = entries * block_scale(stream_key, dims, pieces, -0.22, 0.18)
    return jnp.clip(entries, -most, most).astype(held_as)


def setup_inputs(seed: int = 0) -> dict:
    streams_of = jax.random.split(jax.random.key(seed), 8)
    queries = draw_queries(jax.random.fold_in(streams_of[7], 71), 0)
    comp_kv = draw_comp_kv(jax.random.fold_in(streams_of[7], 71), 0)
    prompt_kv = draw_prompt_kv(jax.random.fold_in(streams_of[7], 71), 0)
    residual = scatter_about(streams_of[3], (PROMPTS, COMPS, CLEN, D), 0.3, 1.796875, ((0, 4), (1, 16), (2, 4)))
    out_weight = scatter_about(streams_of[4], (QH * HD, D), (QH * HD) ** -0.5, 0.125, ((0, 4), (1, 64)))
    gain = jnp.clip(1.0 + 0.18 * jax.random.normal(streams_of[5], (D,), jnp.float32), 0.1, 1.9)
    lengths = draw_lengths(jax.random.fold_in(streams_of[7], 71), 0)
    return {"queries": queries, "comp_kv": comp_kv, "prompt_kv": prompt_kv, "residual": residual, "out_weight": out_weight, "gain": gain, "lengths": lengths}


def rollout_context(query_rows, comp_pairs, prompt_pairs, length):
    groups = QH // KVH
    keys_all = jnp.concatenate([prompt_pairs[:, 0], comp_pairs[:, 0]], axis=0).reshape(PLEN + CLEN, KVH, HD)
    values_all = jnp.concatenate([prompt_pairs[:, 1], comp_pairs[:, 1]], axis=0).reshape(PLEN + CLEN, KVH, HD)
    query_heads = query_rows.reshape(CLEN, KVH, groups, HD)
    scores = jnp.einsum('cgjh,lgh->gjcl', query_heads.astype(jnp.float32), keys_all.astype(jnp.float32)) * HD ** (-0.5)
    positions = jnp.arange(PLEN + CLEN)
    rows_here = jnp.arange(CLEN)
    visible = (positions[None, :] < PLEN) | (positions[None, :] - PLEN <= rows_here[:, None])
    scores = jnp.where(visible, scores, jnp.float32(-1e+30))
    top = lax.optimization_barrier(jnp.max(scores, axis=-1, keepdims=True))
    weights = jnp.exp(scores - top)
    total = lax.optimization_barrier(jnp.sum(weights, axis=-1, keepdims=True))
    rounded = weights.astype(jnp.bfloat16)
    mixed = jnp.einsum('gjcl,lgh->gjch', rounded.astype(jnp.float32), values_all.astype(jnp.float32))
    context = (mixed / total).transpose(2, 0, 1, 3).reshape(CLEN, QH * HD).astype(jnp.bfloat16)
    live = rows_here[:, None] < length
    return jnp.where(live, context, jnp.zeros_like(context))

def reference(queries, comp_kv, prompt_kv, residual, out_weight, gain, lengths):
    block = QH * HD // N_TENSOR
    weight_parts = out_weight.reshape(N_TENSOR, block, D).astype(jnp.float32)

    def one_rollout(index):
        prompt_index = index // COMPS
        completion = index % COMPS
        context = rollout_context(queries[prompt_index, completion], comp_kv[prompt_index, completion], prompt_kv[prompt_index], lengths[prompt_index, completion])
        shares = context.reshape(CLEN, N_TENSOR, block).astype(jnp.float32)
        partial_terms = jnp.einsum('cth,thd->tcd', shares, weight_parts)
        partial_terms = lax.optimization_barrier(partial_terms.astype(jnp.bfloat16)).astype(jnp.float32)
        attended = lax.optimization_barrier(jnp.sum(partial_terms, axis=0)).astype(jnp.bfloat16)
        stream = residual[prompt_index, completion].astype(jnp.float32) + attended.astype(jnp.float32)
        normed = stream * lax.rsqrt(lax.optimization_barrier(jnp.mean(stream * stream, axis=-1, keepdims=True)) + 1e-06) * gain
        return (attended, normed.astype(jnp.bfloat16))
    attended, normed = lax.map(one_rollout, jnp.arange(PROMPTS * COMPS, dtype=jnp.int32))
    return (attended.reshape(PROMPTS, COMPS, CLEN, D), normed.reshape(PROMPTS, COMPS, CLEN, D))
```

```python
import functools

import jax
import jax.numpy as jnp
import numpy as np
from jax import lax
from jax.experimental import pallas as pl
from jax.experimental.pallas import tpu as pltpu
from jax.sharding import PartitionSpec as P

HD = 128
GROUPS = 5
CLEN = 512
PIECE = 256
SCALE = float(HD**-0.5 * np.log2(np.e))
F32 = jnp.float32
BF16 = jnp.bfloat16
NT = (((1,), (1,)), ((), ()))
ANY = pl.BlockSpec(memory_space=pl.ANY)
SMEM = pl.BlockSpec(memory_space=pltpu.SMEM)
VMEM = pl.BlockSpec(memory_space=pltpu.VMEM)
TILE = 128
PARAMS = pltpu.CompilerParams(vmem_limit_bytes=40 << 20)


def absorb(rows, keys, values, top, mixed, mask=None):
    scores = lax.dot_general(rows, keys, NT, preferred_element_type=F32)
    if mask is not None:
        scores = jnp.where(mask, scores, jnp.float32(-1e30))
    best = jnp.max(scores, axis=-1, keepdims=True) * SCALE
    if top is not None:
        best = jnp.maximum(top, best)
    weights = jnp.exp2(scores * SCALE - best).astype(BF16)
    part = jnp.dot(weights, values, preferred_element_type=F32)
    if top is None:
        return best, part
    return best, mixed * jnp.exp2(top - best) + part


def stage(blocks, keys, values, start):
    for block in blocks:
        for j in range(block.shape[0]):
            keys[start : start + PIECE] = block[j, 0]
            values[start : start + PIECE, :HD] = block[j, 1]
            start += PIECE
    return start


def attend_first(query, own, top_out, mixed_out, values):
    @pl.when(pl.program_id(0) == 0)
    def _():
        values[:, :HD] = own[1]
        values[:, HD:] = jnp.ones((CLEN, HD), BF16)

    for r in range(CLEN // TILE):
        extent = (r + 1) * TILE
        column = lax.broadcasted_iota(jnp.int32, (TILE, extent), 1)
        row = lax.broadcasted_iota(jnp.int32, (TILE, extent), 0)
        best, mixed = absorb(
            query[r], own[0, :extent], values[:extent], None, None, column - row <= r * TILE
        )
        top_out[0, r] = jnp.broadcast_to(best, (TILE, HD))
        mixed_out[0, r] = mixed


def attend_more(count, width, query, *refs):
    blocks, (top_in, mixed_in, top_out, mixed_out, keys, values) = refs[:count], refs[count:]

    @pl.when(pl.program_id(0) == 0)
    def _():
        stage(blocks, keys, values, 0)
        values[:, HD:] = jnp.ones((values.shape[0], HD), BF16)

    for r in range(CLEN // TILE):
        best, mixed = top_in[0, r][:, :1], mixed_in[0, r]
        for start in range(0, keys.shape[0], width):
            best, mixed = absorb(
                query[r], keys[start : start + width], values[start : start + width], best, mixed
            )
        top_out[0, r] = jnp.broadcast_to(best, (TILE, HD))
        mixed_out[0, r] = mixed


def attend_last(count, width, half, place, query, *refs):
    blocks, (top_in, mixed_in), outs, (keys, values) = (
        refs[:count],
        refs[count : count + 2],
        refs[count + 2 : -2],
        refs[-2:],
    )
    rows = outs[0].shape[0]
    x, live = place[0], place[3]

    @pl.when(pl.program_id(0) == 0)
    def _():
        stage(blocks, keys, values, 0)
        values[:, HD:] = jnp.ones((values.shape[0], HD), BF16)

    per = TILE // rows
    for d in range(0, 4, per):
        strips = [lax.rem(x + d + i, 4) for i in range(per)]
        best = jnp.concatenate([top_in[0, r] for r in strips], axis=0)[:, :1]
        mixed = jnp.concatenate([mixed_in[0, r] for r in strips], axis=0)
        lines = jnp.concatenate([query[r] for r in strips], axis=0)
        for start in range(0, keys.shape[0], width):
            best, mixed = absorb(
                lines, keys[start : start + width], values[start : start + width], best, mixed
            )
        context = mixed[:, :HD] / mixed[:, HD:]
        line = lax.broadcasted_iota(jnp.int32, (rows, HD), 0)
        for i, r in enumerate(strips):
            kept = jnp.where(
                line + (r * 128 + half * rows) < live, context[i * rows : (i + 1) * rows], 0.0
            )
            outs[d + i][...] = kept.astype(BF16)


def whole(a):
    return pl.BlockSpec(a.shape, lambda h: (0,) * a.ndim)


def cost(rows, keys):
    return pl.CostEstimate(
        flops=24 * rows * keys * HD, bytes_accessed=12 << 20, transcendentals=0
    )


def state_specs(rows, half):
    return [
        pl.BlockSpec((1, 4, rows, HD), lambda h: (h, 0, half, 0)),
        pl.BlockSpec((1, 4, rows, 2 * HD), lambda h: (h, 0, half, 0)),
    ]


STATE = [
    jax.ShapeDtypeStruct((GROUPS, 4, 128, HD), F32),
    jax.ShapeDtypeStruct((GROUPS, 4, 128, 2 * HD), F32),
]


def first_part(query, own):
    return pl.pallas_call(
        attend_first,
        grid=(GROUPS,),
        in_specs=[pl.BlockSpec((4, 128, HD), lambda h: (0, 0, h)), whole(own)],
        out_specs=state_specs(128, 0),
        out_shape=STATE,
        scratch_shapes=[pltpu.VMEM((CLEN, 2 * HD), BF16)],
        compiler_params=PARAMS,
        cost_estimate=cost(GROUPS * CLEN, CLEN),
    )(query, own)


def more_part(query, blocks, state, width):
    extent = sum(b.shape[0] for b in blocks) * PIECE
    return pl.pallas_call(
        functools.partial(attend_more, len(blocks), width),
        grid=(GROUPS,),
        in_specs=[pl.BlockSpec((4, 128, HD), lambda h: (0, 0, h))]
        + [whole(b) for b in blocks]
        + state_specs(128, 0),
        out_specs=state_specs(128, 0),
        out_shape=STATE,
        scratch_shapes=[pltpu.VMEM((extent, HD), BF16), pltpu.VMEM((extent, 2 * HD), BF16)],
        compiler_params=PARAMS,
        cost_estimate=cost(GROUPS * CLEN, extent),
    )(query, *blocks, *state)


def last_part(place, query, blocks, state, width, half, halves):
    extent = sum(b.shape[0] for b in blocks) * PIECE
    rows = 128 // halves
    return pl.pallas_call(
        functools.partial(attend_last, len(blocks), width, half),
        grid=(GROUPS,),
        in_specs=[SMEM, pl.BlockSpec((4, rows, HD), lambda h: (0, half, h))]
        + [whole(b) for b in blocks]
        + state_specs(rows, half),
        out_specs=[pl.BlockSpec((rows, HD), lambda h: (0, h))] * 4,
        out_shape=[jax.ShapeDtypeStruct((rows, GROUPS * HD), BF16)] * 4,
        scratch_shapes=[pltpu.VMEM((extent, HD), BF16), pltpu.VMEM((extent, 2 * HD), BF16)],
        compiler_params=PARAMS,
        cost_estimate=cost(GROUPS * CLEN // halves, extent),
    )(place, query, *blocks, *state)


def project(place, c0, c1, c2, c3, mine, other, o0, o1, o2, o3, held, sems):
    core = place[2]
    copies = []
    for z in range(8):
        for source, parity in ((mine, core), (other, 1 - core)):
            at = pl.multiple_of(z * 160 + parity * 80, 16)
            copies.append(
                pltpu.make_async_copy(
                    source.at[z], held.at[:, pl.ds(at, 80)], sems.at[len(copies)]
                )
            )
    for copy in copies:
        copy.start()
    contexts, outs = (c0, c1, c2, c3), (o0, o1, o2, o3)
    lines = [jnp.concatenate([c[j] for c in contexts], axis=0) for j in range(4)]
    rows = c0.shape[1]
    waited = 0
    for n in range(0, 1280, 256):
        while waited < len(copies) and waited // 2 * 160 < n + 256:
            copies[waited].wait()
            waited += 1
        total = None
        for j in range(4):
            part = lax.dot_general(lines[j], held[j, n : n + 256], NT, preferred_element_type=F32)
            total = part if total is None else total + part
        total = total.astype(BF16)
        for d, out in enumerate(outs):
            out[:, n : n + 256] = total[d * rows : (d + 1) * rows]


def projected(place, contexts, mine, other):
    rows = contexts[0].shape[1]
    block = jax.ShapeDtypeStruct((rows, 1280), BF16)
    return pl.pallas_call(
        project,
        in_specs=[SMEM] + [VMEM] * 4 + [ANY] * 2,
        out_specs=[VMEM] * 4,
        out_shape=[block] * 4,
        scratch_shapes=[pltpu.VMEM((4, 1280, 640), BF16), pltpu.SemaphoreType.DMA((16,))],
        compiler_params=PARAMS,
        cost_estimate=pl.CostEstimate(
            flops=rows * 2560 * 1280 // 4, bytes_accessed=1 << 20, transcendentals=0
        ),
    )(place, *contexts, mine, other)


def finish(place, *refs):
    count = (len(refs) - 4) // 4
    residual, gain, attended, normed = refs[-4:]
    y = place[1]
    for h in range(count):
        rows = refs[4 * h].shape[0]
        for d in range(4):
            at = pl.multiple_of(lax.rem(y + d, 4) * 1280, 1280)
            attended[h * rows : (h + 1) * rows, pl.ds(at, 1280)] = refs[4 * h + d][...]
    for r in range(0, 128, 16):
        stream = residual[r : r + 16].astype(F32) + attended[r : r + 16].astype(F32)
        power = jnp.mean(stream * stream, axis=-1, keepdims=True)
        normed[r : r + 16] = (stream * lax.rsqrt(power + 1e-06) * gain[...]).astype(BF16)


def finished(place, parts, residual, gain):
    block = jax.ShapeDtypeStruct((128, 5120), BF16)
    return pl.pallas_call(
        finish,
        in_specs=[SMEM] + [VMEM] * (len(parts) + 2),
        out_specs=[VMEM] * 2,
        out_shape=[block] * 2,
        compiler_params=PARAMS,
    )(place, *parts, residual, gain)


UP = [(i, (i + 1) % 4) for i in range(4)]
DOWN = [(i, (i - 1) % 4) for i in range(4)]
ACROSS = [(i, (i + 2) % 4) for i in range(4)]
SWAP = [(i, i ^ 1) for i in range(16)]
EACH_CORE = [list(range(0, 16, 2)), list(range(1, 16, 2))]


def along(distance):
    return [
        (g, (g // 2 + (distance if g % 2 == 0 else -distance)) % 8 * 2 + g % 2) for g in range(16)
    ]


def around(axis, down, across, up):
    return [
        lax.ppermute(down, axis, DOWN),
        lax.ppermute(across, axis, ACROSS),
        lax.ppermute(up, axis, UP),
    ]


def after(value, *others):
    return lax.optimization_barrier((value, *others))[0]


def shards(queries, comp_kv, prompt_kv, residual, out_weight, gain, lengths):
    x, y, group = lax.axis_index("tensor"), lax.axis_index("dp"), lax.axis_index("group")
    place = jnp.stack([x, y, group % 2, lengths[0, 0]]).astype(jnp.int32)
    query = queries[0, 0].reshape(4, 128, GROUPS * HD)
    swap = functools.partial(lax.ppermute, axis_name="group", perm=SWAP)

    with jax.named_scope("prompt"):
        piece = prompt_kv[0].transpose(1, 0, 2)[None]
        pair = jnp.concatenate([piece, swap(piece)], axis=0)

    weight = out_weight.T
    with jax.named_scope("weights"):
        weight = after(weight, pair)
        pieces = jnp.stack([weight] + around("tensor", weight, weight, weight))
        mine = lax.all_gather(pieces, "group", axis=0, axis_index_groups=EACH_CORE)

    with jax.named_scope("attention"):
        own = comp_kv[0, 0].transpose(1, 0, 2)
        state = first_part(query, own)
        come, late = pair, pair
        for step in range(3):
            come = after(lax.ppermute(come, "group", along(1)), *state)
            state = more_part(query, [late, come], state, 1024)
            late = swap(come)
        come = after(lax.ppermute(come[:1], "group", along(1)), *state)
        c0, c1, c2, c3 = last_part(place, query, [late, come, swap(come)], state, 1024, 0, 1)

    with jax.named_scope("exchange"):
        blocks = [c0] + around("tensor", c3, c2, c1)
        halves = 2
        rows = 128 // halves
        contexts = []
        for half in range(halves):
            mixed = jnp.stack([a[half * rows : (half + 1) * rows] for a in blocks])
            contexts.append([mixed] + around("dp", mixed, mixed, mixed))

    with jax.named_scope("weights"):
        mine = after(mine, contexts[0][0])
        other = swap(mine)
    parts = []
    for half in range(halves):
        with jax.named_scope("project"):
            o0, o1, o2, o3 = projected(place, contexts[half], mine, other)
            parts += [o0] + around("dp", o3, o2, o1)
    with jax.named_scope("finish"):
        attended, normed = finished(place, parts, residual[0, 0], gain[None])
    return (attended[None, None], normed[None, None])


def solution(mesh):
    in_specs = (
        P("dp", "group", None, "tensor"),
        P("dp", "group", None, None, "tensor"),
        P("dp", "group", None, "tensor"),
        P("dp", "group", "tensor", None),
        P("tensor", ("dp", "group")),
        P(),
        P("dp", "group"),
    )
    out_specs = (P("dp", "group", "tensor", None), P("dp", "group", "tensor", None))
    return jax.shard_map(shards, mesh=mesh, in_specs=in_specs, out_specs=out_specs, check_vma=False)
```

```python
import functools

import jax
import jax.numpy as jnp
import numpy as np
from jax import lax
from jax.experimental import pallas as pl
from jax.experimental.pallas import tpu as pltpu
from jax.sharding import PartitionSpec as P

HD = 128
GROUPS = 5
CLEN = 512
PIECE = 256
SCALE = float(HD**-0.5 * np.log2(np.e))
F32 = jnp.float32
BF16 = jnp.bfloat16
NT = (((1,), (1,)), ((), ()))
ANY = pl.BlockSpec(memory_space=pl.ANY)
SMEM = pl.BlockSpec(memory_space=pltpu.SMEM)
VMEM = pl.BlockSpec(memory_space=pltpu.VMEM)
TILE = 256
PARAMS = pltpu.CompilerParams(vmem_limit_bytes=20 << 20)


def absorb(rows, keys, values, top, mixed, mask=None):
    scores = lax.dot_general(rows, keys, NT, preferred_element_type=F32)
    if mask is not None:
        scores = jnp.where(mask, scores, jnp.float32(-1e30))
    best = jnp.max(scores, axis=-1, keepdims=True) * SCALE
    if top is not None:
        best = jnp.maximum(top, best)
    weights = jnp.exp2(scores * SCALE - best).astype(BF16)
    part = jnp.dot(weights, values, preferred_element_type=F32)
    if top is None:
        return best, part
    return best, mixed * jnp.exp2(top - best) + part


def load_state(top, mixed):
    total = jnp.broadcast_to(top[:, HD // 2 : HD // 2 + 1], mixed.shape)
    return top[:, :1], jnp.concatenate([mixed, total], axis=1)


def store_state(best, mixed):
    low = lax.broadcasted_iota(jnp.int32, mixed[:, :HD].shape, 1) < HD // 2
    return jnp.where(low, best, mixed[:, HD:]), mixed[:, :HD]


def stage(blocks, keys, values, start):
    for block in blocks:
        for j in range(block.shape[0]):
            keys[start : start + PIECE] = block[j, 0]
            values[start : start + PIECE, :HD] = block[j, 1]
            start += PIECE
    return start


def head(query, r, h):
    return query[r : r + TILE, h * HD : (h + 1) * HD]


def attend_first(count, query, own, *refs):
    blocks, (top_out, mixed_out, token, keys, values) = refs[:count], refs[count:]
    token[...] = jnp.zeros_like(token)
    prompt = stage(blocks, keys, values, 0)
    keys[prompt:] = own[0]
    values[prompt:, :HD] = own[1]
    values[:, HD:] = jnp.ones((values.shape[0], HD), BF16)

    for h in range(GROUPS):
        for r in range(0, CLEN, TILE):
            lines = head(query, r, h)
            best, mixed = absorb(lines, keys[:1024], values[:1024], None, None)
            extent = prompt + r + TILE - 1024
            column = lax.broadcasted_iota(jnp.int32, (TILE, extent), 1)
            row = lax.broadcasted_iota(jnp.int32, (TILE, extent), 0)
            best, mixed = absorb(
                lines,
                keys[1024 : 1024 + extent],
                values[1024 : 1024 + extent],
                best,
                mixed,
                column - row <= extent - TILE,
            )
            top_out[h, r : r + TILE], mixed_out[h, r : r + TILE] = store_state(best, mixed)


def attend_more(count, query, *refs):
    blocks, (top_in, mixed_in, top_out, mixed_out, token, keys, values) = (
        refs[:count],
        refs[count:],
    )
    token[...] = jnp.zeros_like(token)
    stage(blocks, keys, values, 0)
    values[:, HD:] = jnp.ones((values.shape[0], HD), BF16)

    for h in range(GROUPS):
        for r in range(0, CLEN, TILE):
            best, mixed = load_state(top_in[h, r : r + TILE], mixed_in[h, r : r + TILE])
            best, mixed = absorb(head(query, r, h), keys[...], values[...], best, mixed)
            top_out[h, r : r + TILE], mixed_out[h, r : r + TILE] = store_state(best, mixed)


def attend_last(count, place, query, *refs):
    blocks, (top_in, mixed_in, o0, o1, o2, o3, context, keys, values) = (
        refs[:count],
        refs[count:],
    )
    x, live = place[0], place[3]
    stage(blocks, keys, values, 0)
    values[:, HD:] = jnp.ones((values.shape[0], HD), BF16)

    for h in range(GROUPS):
        best, mixed = load_state(top_in[h], mixed_in[h])
        lines = query[:, h * HD : (h + 1) * HD]
        best, mixed = absorb(lines, keys[...], values[...], best, mixed)
        line = lax.broadcasted_iota(jnp.int32, (CLEN, HD), 0)
        context[:, h * HD : (h + 1) * HD] = jnp.where(
            line < live, mixed[:, :HD] / mixed[:, HD:], 0.0
        ).astype(BF16)
    for d, out in enumerate((o0, o1, o2, o3)):
        out[...] = context[pl.ds(pl.multiple_of(lax.rem(x + d, 4) * 128, 128), 128)]


def cost(rows, keys):
    return pl.CostEstimate(
        flops=24 * rows * keys * HD, bytes_accessed=12 << 20, transcendentals=0
    )


STATE = [jax.ShapeDtypeStruct((GROUPS, CLEN, HD), F32)] * 2
TOKEN = jax.ShapeDtypeStruct((8, HD), F32)


def room(blocks, more=0):
    extent = sum(b.shape[0] for b in blocks) * PIECE + more
    return [pltpu.VMEM((extent, HD), BF16), pltpu.VMEM((extent, 2 * HD), BF16)]


def first_part(query, own, blocks):
    return pl.pallas_call(
        functools.partial(attend_first, len(blocks)),
        in_specs=[VMEM] * (2 + len(blocks)),
        out_specs=[VMEM] * 3,
        out_shape=[pltpu.HBM(s.shape, s.dtype) for s in STATE] + [TOKEN],
        scratch_shapes=room(blocks, CLEN),
        compiler_params=PARAMS,
        cost_estimate=cost(GROUPS * CLEN, 2048),
    )(query, own, *blocks)


def more_part(query, blocks, state):
    return pl.pallas_call(
        functools.partial(attend_more, len(blocks)),
        in_specs=[VMEM] * (3 + len(blocks)),
        out_specs=[VMEM] * 3,
        out_shape=STATE + [TOKEN],
        scratch_shapes=room(blocks),
        compiler_params=PARAMS,
        cost_estimate=cost(GROUPS * CLEN, 1024),
    )(query, *blocks, *state)


def last_part(place, query, blocks, state):
    return pl.pallas_call(
        functools.partial(attend_last, len(blocks)),
        in_specs=[SMEM] + [VMEM] * (3 + len(blocks)),
        out_specs=[VMEM] * 4,
        out_shape=[jax.ShapeDtypeStruct((128, GROUPS * HD), BF16)] * 4,
        scratch_shapes=[pltpu.VMEM((CLEN, GROUPS * HD), BF16)] + room(blocks),
        compiler_params=PARAMS,
        cost_estimate=cost(GROUPS * CLEN, 1024),
    )(place, query, *blocks, *state)


def whole(a):
    return pl.BlockSpec(a.shape, lambda h: (0,) * a.ndim)


def gate(value, *refs):
    refs[-1][...] = value[...]


def gated(value, ready):
    return pl.pallas_call(
        gate,
        in_specs=[VMEM, ANY],
        out_specs=VMEM,
        out_shape=jax.ShapeDtypeStruct(value.shape, value.dtype),
        compiler_params=PARAMS,
    )(value, ready)


def widen(b0, b1, b2, b3, *refs):
    out = refs[-1]
    for j, block in enumerate((b0, b1, b2, b3)):
        out[:, j * 640 : (j + 1) * 640] = block[...]


def widened(blocks, *ready):
    return pl.pallas_call(
        widen,
        in_specs=[VMEM] * 4 + [ANY] * len(ready),
        out_specs=VMEM,
        out_shape=jax.ShapeDtypeStruct((80, 2560), BF16),
        compiler_params=PARAMS,
    )(*blocks, *ready)


def pack(place, *refs):
    blocks, out = refs[:-1], refs[-1]
    out[0] = blocks[0][...]
    for i in range(1, 4):
        out[i] = blocks[i][...]
    if len(blocks) > 4:

        @pl.when(place[2] == 1)
        def _():
            for i in range(1, 4):
                out[i] = blocks[i + 3][...]


def packed(place, *blocks):
    return pl.pallas_call(
        pack,
        in_specs=[SMEM] + [VMEM] * len(blocks),
        out_specs=VMEM,
        out_shape=jax.ShapeDtypeStruct((4, *blocks[0].shape), BF16),
        compiler_params=PARAMS,
    )(place, *blocks)


def project(place, c0, c1, c2, c3, columns, o0, o1, o2, o3, lines):
    contexts, outs = (c0, c1, c2, c3), (o0, o1, o2, o3)
    rows, depth = c0.shape[1:]

    def lay(pick):
        for d in range(4):
            for j in range(4):
                lines[d * rows : (d + 1) * rows, j * depth : (j + 1) * depth] = pick(d, j)

    @pl.when((pl.program_id(0) == 0) & (place[2] == 0))
    def _():
        lay(lambda d, j: contexts[j][(d - j) % 4])

    @pl.when((pl.program_id(0) == 0) & (place[2] == 1))
    def _():
        lay(lambda d, j: contexts[d][j])

    total = lax.dot_general(lines[...], columns[...], NT, preferred_element_type=F32)
    total = total.astype(BF16)
    for d, out in enumerate(outs):
        out[...] = total[d * rows : (d + 1) * rows]


def projected(place, contexts, columns):
    rows = contexts[0].shape[1]
    block = jax.ShapeDtypeStruct((rows, 1280), BF16)
    return pl.pallas_call(
        project,
        grid=(5,),
        in_specs=[SMEM]
        + [whole(c) for c in contexts]
        + [pl.BlockSpec((256, 2560), lambda n: (n, 0))],
        out_specs=[pl.BlockSpec((rows, 256), lambda n: (0, n))] * 4,
        out_shape=[block] * 4,
        scratch_shapes=[pltpu.VMEM((4 * rows, 2560), BF16)],
        compiler_params=pltpu.CompilerParams(vmem_limit_bytes=60 << 20),
        cost_estimate=pl.CostEstimate(
            flops=2 * 4 * rows * 2560 * 1280, bytes_accessed=10 << 20, transcendentals=0
        ),
    )(place, *contexts, columns)


def finish(place, p0, p1, p2, p3, residual, gain, attended, normed):
    quarter = place[0] + place[1]
    for d, part in enumerate((p0, p1, p2, p3)):
        at = pl.multiple_of(lax.rem(quarter + d, 4) * 1280, 1280)
        attended[:, pl.ds(at, 1280)] = part[...]
    for r in range(0, residual.shape[0], 16):
        stream = residual[r : r + 16].astype(F32) + attended[r : r + 16].astype(F32)
        power = jnp.mean(stream * stream, axis=-1, keepdims=True)
        normed[r : r + 16] = (stream * lax.rsqrt(power + 1e-06) * gain[...]).astype(BF16)


def finished(place, parts, residual, gain):
    block = jax.ShapeDtypeStruct((128, 5120), BF16)
    lines = 32
    wide = pl.BlockSpec((lines, 5120), lambda n: (n, 0))
    return pl.pallas_call(
        finish,
        grid=(128 // lines,),
        in_specs=[SMEM]
        + [pl.BlockSpec((lines, 1280), lambda n: (n, 0))] * 4
        + [wide, pl.BlockSpec((1, 5120), lambda n: (0, 0))],
        out_specs=[wide] * 2,
        out_shape=[block] * 2,
        compiler_params=PARAMS,
    )(place, *parts, residual, gain)


SWAP = [(i, i ^ 1) for i in range(16)]


def along(distance):
    return [
        (g, (g // 2 + (distance if g % 2 == 0 else -distance)) % 8 * 2 + g % 2) for g in range(16)
    ]


EVERY = ("dp", "group", "tensor")


def ring(step):
    pairs = []
    for y in range(4):
        for g in range(16):
            for x in range(4):
                to = (y, (x + step) % 4) if g % 2 == 0 else ((y + step) % 4, x)
                pairs.append(((y * 16 + g) * 4 + x, (to[0] * 16 + g) * 4 + to[1]))
    return pairs


SLANT = [(y * 4 + x, (y - x) % 4 * 4 + x) for y in range(4) for x in range(4)]


def around(axes, ways, behind, across, ahead):
    return [
        lax.ppermute(a, axes, way)
        for a, way in zip((behind, across, ahead), (ways(-1), ways(2), ways(1)))
    ]


def plain(step):
    return [(i, (i + step) % 4) for i in range(4)]


def shards(queries, comp_kv, prompt_kv, residual, out_weight, gain, lengths):
    x, y, group = lax.axis_index("tensor"), lax.axis_index("dp"), lax.axis_index("group")
    place = jnp.stack([x, y, group % 2, lengths[0, 0]]).astype(jnp.int32)
    query = queries[0, 0]
    swap = functools.partial(lax.ppermute, axis_name="group", perm=SWAP)

    with jax.named_scope("prompt"):
        piece = prompt_kv[0].transpose(1, 0, 2)[None]
        pair = jnp.concatenate([piece, swap(piece)], axis=0)

    weight = out_weight.T
    own = comp_kv[0, 0].transpose(1, 0, 2)
    with jax.named_scope("weights"):
        pieces = around("tensor", plain, weight, weight, weight)
        wide = widened([weight, *pieces])
        pieces = lax.ppermute(wide, ("dp", "tensor"), SLANT)
    with jax.named_scope("attention"):
        z1 = gated(lax.ppermute(pair, "group", along(1)), wide)
        z2 = lax.ppermute(z1, "group", along(1))
        *state, token = first_part(query, own, [pair, z1, swap(z1)])
        z2 = gated(z2, token)
    with jax.named_scope("weights"):
        columns = lax.all_gather(gated(pieces, z2), "group", axis=0, tiled=True)
    with jax.named_scope("attention"):
        z3 = lax.ppermute(z2, "group", along(1))
        *state, token = more_part(query, [z2, swap(z2)], state)
        z3 = gated(z3, token)
        z4 = lax.ppermute(z3[:1], "group", along(1))
        *state, token = more_part(query, [z3, swap(z3)], state)
        z4 = gated(z4, token)
        c0, c1, c2, c3 = last_part(place, query, [z4, swap(z4)], state)

    with jax.named_scope("exchange"):
        blocks = around("tensor", plain, c3, c2, c1)
        mixed = packed(place, c0, c1, c2, c3, *blocks)
        contexts = [mixed] + around(EVERY, ring, mixed, mixed, mixed)

    with jax.named_scope("project"):
        o0, o1, o2, o3 = projected(place, contexts, columns)
        parts = [o0] + around(EVERY, ring, o3, o2, o1)
    with jax.named_scope("finish"):
        attended, normed = finished(place, parts, residual[0, 0], gain[None])
    return (attended[None, None], normed[None, None])


def solution(mesh):
    in_specs = (
        P("dp", "group", None, "tensor"),
        P("dp", "group", None, None, "tensor"),
        P("dp", "group", None, "tensor"),
        P("dp", "group", "tensor", None),
        P("tensor", ("dp", "group")),
        P(),
        P("dp", "group"),
    )
    out_specs = (P("dp", "group", "tensor", None), P("dp", "group", "tensor", None))
    return jax.shard_map(shards, mesh=mesh, in_specs=in_specs, out_specs=out_specs, check_vma=False)
```

```python
import functools

import jax
import jax.numpy as jnp
import numpy as np
from jax import lax
from jax.experimental import pallas as pl
from jax.experimental.pallas import tpu as pltpu
from jax.sharding import PartitionSpec as P

HD = 128
GROUPS = 5
CLEN = 512
PIECE = 256
SCALE = float(HD**-0.5 * np.log2(np.e))
F32 = jnp.float32
BF16 = jnp.bfloat16
NT = (((1,), (1,)), ((), ()))
ANY = pl.BlockSpec(memory_space=pl.ANY)
SMEM = pl.BlockSpec(memory_space=pltpu.SMEM)
VMEM = pl.BlockSpec(memory_space=pltpu.VMEM)
TILE = 256
PARAMS = pltpu.CompilerParams(vmem_limit_bytes=20 << 20)


def absorb(rows, keys, values, top, mixed, mask=None):
    scores = lax.dot_general(rows, keys, NT, preferred_element_type=F32)
    if mask is not None:
        scores = jnp.where(mask, scores, jnp.float32(-1e30))
    best = jnp.max(scores, axis=-1, keepdims=True) * SCALE
    if top is not None:
        best = jnp.maximum(top, best)
    weights = jnp.exp2(scores * SCALE - best).astype(BF16)
    part = jnp.dot(weights, values, preferred_element_type=F32)
    if top is None:
        return best, part
    return best, mixed * jnp.exp2(top - best) + part


def load_state(top, mixed):
    total = jnp.broadcast_to(top[:, HD // 2 : HD // 2 + 1], mixed.shape)
    return top[:, :1], jnp.concatenate([mixed, total], axis=1)


def store_state(best, mixed):
    low = lax.broadcasted_iota(jnp.int32, mixed[:, :HD].shape, 1) < HD // 2
    return jnp.where(low, best, mixed[:, HD:]), mixed[:, :HD]


def stage(blocks, keys, values, start):
    for block in blocks:
        for j in range(block.shape[0]):
            keys[start : start + PIECE] = block[j, 0]
            values[start : start + PIECE, :HD] = block[j, 1]
            start += PIECE
    return start


def head(query, r, h):
    return query[r : r + TILE, h * HD : (h + 1) * HD]


def attend_first(count, query, own, *refs):
    blocks, (top_out, mixed_out, token, keys, values) = refs[:count], refs[count:]
    token[...] = jnp.zeros_like(token)
    prompt = stage(blocks, keys, values, 0)
    keys[prompt:] = own[0]
    values[prompt:, :HD] = own[1]
    values[:, HD:] = jnp.ones((values.shape[0], HD), BF16)

    for h in range(GROUPS):
        for r in range(0, CLEN, TILE):
            lines = head(query, r, h)
            extent = prompt + r + TILE
            column = lax.broadcasted_iota(jnp.int32, (TILE, extent), 1)
            row = lax.broadcasted_iota(jnp.int32, (TILE, extent), 0)
            best, mixed = absorb(
                lines, keys[:extent], values[:extent], None, None, column - row <= extent - TILE
            )
            top_out[h, r : r + TILE], mixed_out[h, r : r + TILE] = store_state(best, mixed)


def attend_more(count, width, query, *refs):
    blocks, (top_in, mixed_in, top_out, mixed_out, token, keys, values) = (
        refs[:count],
        refs[count:],
    )
    token[...] = jnp.zeros_like(token)
    stage(blocks, keys, values, 0)
    values[:, HD:] = jnp.ones((values.shape[0], HD), BF16)

    for h in range(GROUPS):
        for r in range(0, CLEN, TILE):
            best, mixed = load_state(top_in[h, r : r + TILE], mixed_in[h, r : r + TILE])
            for at in range(0, keys.shape[0], width):
                best, mixed = absorb(
                    head(query, r, h), keys[at : at + width], values[at : at + width], best, mixed
                )
            top_out[h, r : r + TILE], mixed_out[h, r : r + TILE] = store_state(best, mixed)


def attend_last(count, place, query, *refs):
    blocks, (top_in, mixed_in, o0, o1, o2, o3, context, keys, values) = (
        refs[:count],
        refs[count:],
    )
    x, live = place[0], place[3]
    stage(blocks, keys, values, 0)
    values[:, HD:] = jnp.ones((values.shape[0], HD), BF16)

    for h in range(GROUPS):
        for r in range(0, CLEN, TILE):
            best, mixed = load_state(top_in[h, r : r + TILE], mixed_in[h, r : r + TILE])
            best, mixed = absorb(head(query, r, h), keys[...], values[...], best, mixed)
            line = lax.broadcasted_iota(jnp.int32, (TILE, HD), 0) + r
            context[r : r + TILE, h * HD : (h + 1) * HD] = jnp.where(
                line < live, mixed[:, :HD] / mixed[:, HD:], 0.0
            ).astype(BF16)
    for d, out in enumerate((o0, o1, o2, o3)):
        out[...] = context[pl.ds(pl.multiple_of(lax.rem(x + d, 4) * 128, 128), 128)]


def cost(rows, keys):
    return pl.CostEstimate(
        flops=24 * rows * keys * HD, bytes_accessed=12 << 20, transcendentals=0
    )


STATE = [jax.ShapeDtypeStruct((GROUPS, CLEN, HD), F32)] * 2
TOKEN = jax.ShapeDtypeStruct((8, HD), F32)


def room(blocks, more=0):
    extent = sum(b.shape[0] for b in blocks) * PIECE + more
    return [pltpu.VMEM((extent, HD), BF16), pltpu.VMEM((extent, 2 * HD), BF16)]


def first_part(query, own, blocks):
    return pl.pallas_call(
        functools.partial(attend_first, len(blocks)),
        in_specs=[VMEM] * (2 + len(blocks)),
        out_specs=[VMEM] * 3,
        out_shape=STATE + [TOKEN],
        scratch_shapes=room(blocks, CLEN),
        compiler_params=PARAMS,
        cost_estimate=cost(GROUPS * CLEN, 2048),
    )(query, own, *blocks)


def more_part(query, blocks, state, width, leave=False):
    return pl.pallas_call(
        functools.partial(attend_more, len(blocks), width),
        in_specs=[VMEM] * (3 + len(blocks)),
        out_specs=[VMEM] * 3,
        out_shape=([pltpu.HBM(s.shape, s.dtype) for s in STATE] if leave else STATE) + [TOKEN],
        scratch_shapes=room(blocks),
        compiler_params=PARAMS,
        cost_estimate=cost(GROUPS * CLEN, 1024),
    )(query, *blocks, *state)


def last_part(place, query, blocks, state):
    return pl.pallas_call(
        functools.partial(attend_last, len(blocks)),
        in_specs=[SMEM] + [VMEM] * (3 + len(blocks)),
        out_specs=[VMEM] * 4,
        out_shape=[jax.ShapeDtypeStruct((128, GROUPS * HD), BF16)] * 4,
        scratch_shapes=[pltpu.VMEM((CLEN, GROUPS * HD), BF16)] + room(blocks),
        compiler_params=PARAMS,
        cost_estimate=cost(GROUPS * CLEN, 1024),
    )(place, query, *blocks, *state)


def whole(a):
    return pl.BlockSpec(a.shape, lambda h: (0,) * a.ndim)


def gate(value, *refs):
    refs[-1][...] = value[...]


def gated(value, ready):
    return pl.pallas_call(
        gate,
        in_specs=[VMEM, ANY],
        out_specs=VMEM,
        out_shape=jax.ShapeDtypeStruct(value.shape, value.dtype),
        compiler_params=PARAMS,
    )(value, ready)


def widen(b0, b1, b2, b3, *refs):
    out = refs[-1]
    for j, block in enumerate((b0, b1, b2, b3)):
        out[:, j * 640 : (j + 1) * 640] = block[...]


def widened(blocks, *ready):
    return pl.pallas_call(
        widen,
        in_specs=[VMEM] * 4 + [ANY] * len(ready),
        out_specs=VMEM,
        out_shape=jax.ShapeDtypeStruct((80, 2560), BF16),
        compiler_params=PARAMS,
    )(*blocks, *ready)


def pack(place, *refs):
    blocks, out = refs[:-1], refs[-1]
    out[0] = blocks[0][...]
    for i in range(1, 4):
        out[i] = blocks[i][...]
    if len(blocks) > 4:

        @pl.when(place[2] == 1)
        def _():
            for i in range(1, 4):
                out[i] = blocks[i + 3][...]


def packed(place, *blocks):
    return pl.pallas_call(
        pack,
        in_specs=[SMEM] + [VMEM] * len(blocks),
        out_specs=VMEM,
        out_shape=jax.ShapeDtypeStruct((4, *blocks[0].shape), BF16),
        compiler_params=PARAMS,
    )(place, *blocks)


def project(place, c0, c1, c2, c3, columns, o0, o1, o2, o3, lines):
    contexts, outs = (c0, c1, c2, c3), (o0, o1, o2, o3)
    rows, depth = c0.shape[1:]

    def lay(pick):
        for d in range(4):
            for j in range(4):
                lines[d * rows : (d + 1) * rows, j * depth : (j + 1) * depth] = pick(d, j)

    @pl.when((pl.program_id(0) == 0) & (place[2] == 0))
    def _():
        lay(lambda d, j: contexts[j][(d - j) % 4])

    @pl.when((pl.program_id(0) == 0) & (place[2] == 1))
    def _():
        lay(lambda d, j: contexts[d][j])

    total = lax.dot_general(lines[...], columns[...], NT, preferred_element_type=F32)
    total = total.astype(BF16)
    for d, out in enumerate(outs):
        out[...] = total[d * rows : (d + 1) * rows]


def projected(place, contexts, columns):
    rows = contexts[0].shape[1]
    block = jax.ShapeDtypeStruct((rows, 1280), BF16)
    return pl.pallas_call(
        project,
        grid=(5,),
        in_specs=[SMEM]
        + [whole(c) for c in contexts]
        + [pl.BlockSpec((256, 2560), lambda n: (n, 0))],
        out_specs=[pl.BlockSpec((rows, 256), lambda n: (0, n))] * 4,
        out_shape=[block] * 4,
        scratch_shapes=[pltpu.VMEM((4 * rows, 2560), BF16)],
        compiler_params=pltpu.CompilerParams(vmem_limit_bytes=24 << 20),
        cost_estimate=pl.CostEstimate(
            flops=2 * 4 * rows * 2560 * 1280, bytes_accessed=10 << 20, transcendentals=0
        ),
    )(place, *contexts, columns)


def finish(place, p0, p1, p2, p3, residual, gain, attended, normed):
    quarter = place[0] + place[1]
    for d, part in enumerate((p0, p1, p2, p3)):
        at = pl.multiple_of(lax.rem(quarter + d, 4) * 1280, 1280)
        attended[:, pl.ds(at, 1280)] = part[...]
    for r in range(0, residual.shape[0], 16):
        stream = residual[r : r + 16].astype(F32) + attended[r : r + 16].astype(F32)
        power = jnp.mean(stream * stream, axis=-1, keepdims=True)
        normed[r : r + 16] = (stream * lax.rsqrt(power + 1e-06) * gain[...]).astype(BF16)


def finished(place, parts, residual, gain):
    block = jax.ShapeDtypeStruct((128, 5120), BF16)
    lines = 32
    wide = pl.BlockSpec((lines, 5120), lambda n: (n, 0))
    return pl.pallas_call(
        finish,
        grid=(128 // lines,),
        in_specs=[SMEM]
        + [pl.BlockSpec((lines, 1280), lambda n: (n, 0))] * 4
        + [wide, pl.BlockSpec((1, 5120), lambda n: (0, 0))],
        out_specs=[wide] * 2,
        out_shape=[block] * 2,
        compiler_params=PARAMS,
    )(place, *parts, residual, gain)


SWAP = [(i, i ^ 1) for i in range(16)]


def along(distance):
    return [
        (g, (g // 2 + (distance if g % 2 == 0 else -distance)) % 8 * 2 + g % 2) for g in range(16)
    ]


EVERY = ("dp", "group", "tensor")


def ring(step):
    pairs = []
    for y in range(4):
        for g in range(16):
            for x in range(4):
                to = (y, (x + step) % 4) if g % 2 == 0 else ((y + step) % 4, x)
                pairs.append(((y * 16 + g) * 4 + x, (to[0] * 16 + g) * 4 + to[1]))
    return pairs


SLANT = [(y * 4 + x, (y - x) % 4 * 4 + x) for y in range(4) for x in range(4)]


def around(axes, ways, behind, across, ahead):
    return [
        lax.ppermute(a, axes, way)
        for a, way in zip((behind, across, ahead), (ways(-1), ways(2), ways(1)))
    ]


def plain(step):
    return [(i, (i + step) % 4) for i in range(4)]


def kept(state):
    return [pltpu.with_memory_space_constraint(a, pltpu.HBM) for a in state]


def shards(queries, comp_kv, prompt_kv, residual, out_weight, gain, lengths):
    x, y, group = lax.axis_index("tensor"), lax.axis_index("dp"), lax.axis_index("group")
    place = jnp.stack([x, y, group % 2, lengths[0, 0]]).astype(jnp.int32)
    query = queries[0, 0]
    swap = functools.partial(lax.ppermute, axis_name="group", perm=SWAP)

    with jax.named_scope("prompt"):
        piece = prompt_kv[0].transpose(1, 0, 2)[None]
        pair = jnp.concatenate([piece, swap(piece)], axis=0)

    weight = out_weight.T
    own = comp_kv[0, 0].transpose(1, 0, 2)
    with jax.named_scope("weights"):
        pieces = around("tensor", plain, weight, weight, weight)
    with jax.named_scope("attention"):
        z1 = lax.ppermute(pair, "group", along(1))
        *state, token = first_part(query, own, [pair])
    with jax.named_scope("weights"):
        wide = widened([weight, *pieces], token)
        pieces = lax.ppermute(wide, ("dp", "tensor"), SLANT)
    with jax.named_scope("attention"):
        z1 = gated(z1, wide)
        z2 = lax.ppermute(z1, "group", along(1))
        z4 = lax.ppermute(z1[:1], "group", along(3))
        *state, token = more_part(query, [z1, swap(z1)], state, 1024, True)
        z2 = gated(z2, token)
        z4 = gated(z4, z2)
    with jax.named_scope("weights"):
        columns = lax.all_gather(gated(pieces, z4), "group", axis=0, tiled=True)
    with jax.named_scope("attention"):
        z3 = lax.ppermute(z2, "group", along(1))
        *state, token = more_part(
            query, [z2, z4, swap(z2), swap(z4)], kept(state), 1536, True
        )
        z3 = gated(z3, token)
        c0, c1, c2, c3 = last_part(place, query, [z3, swap(z3)], kept(state))

    with jax.named_scope("exchange"):
        blocks = around("tensor", plain, c3, c2, c1)
        mixed = packed(place, c0, c1, c2, c3, *blocks)
        contexts = [mixed] + around(EVERY, ring, mixed, mixed, mixed)

    with jax.named_scope("project"):
        o0, o1, o2, o3 = projected(
            place, contexts, pltpu.with_memory_space_constraint(columns, pltpu.HBM)
        )
        parts = [o0] + around(EVERY, ring, o3, o2, o1)
    with jax.named_scope("finish"):
        attended, normed = finished(place, parts, residual[0, 0], gain[None])
    return (attended[None, None], normed[None, None])


def solution(mesh):
    in_specs = (
        P("dp", "group", None, "tensor"),
        P("dp", "group", None, None, "tensor"),
        P("dp", "group", None, "tensor"),
        P("dp", "group", "tensor", None),
        P("tensor", ("dp", "group")),
        P(),
        P("dp", "group"),
    )
    out_specs = (P("dp", "group", "tensor", None), P("dp", "group", "tensor", None))
    return jax.shard_map(shards, mesh=mesh, in_specs=in_specs, out_specs=out_specs, check_vma=False)
```

```python
import functools

import jax
import jax.numpy as jnp
import numpy as np
from jax import lax
from jax.experimental import pallas as pl
from jax.experimental.pallas import tpu as pltpu
from jax.sharding import PartitionSpec as P

HD = 128
GROUPS = 5
CLEN = 512
PIECE = 256
SCALE = float(HD**-0.5 * np.log2(np.e))
F32 = jnp.float32
BF16 = jnp.bfloat16
NT = (((1,), (1,)), ((), ()))
ANY = pl.BlockSpec(memory_space=pl.ANY)
SMEM = pl.BlockSpec(memory_space=pltpu.SMEM)
VMEM = pl.BlockSpec(memory_space=pltpu.VMEM)
TILE = 256
PARAMS = pltpu.CompilerParams(vmem_limit_bytes=20 << 20)


def absorb(rows, keys, values, top, mixed, mask=None):
    scores = lax.dot_general(rows, keys, NT, preferred_element_type=F32)
    if mask is not None:
        scores = jnp.where(mask, scores, jnp.float32(-1e30))
    best = jnp.max(scores, axis=-1, keepdims=True) * SCALE
    if top is not None:
        best = jnp.maximum(top, best)
    weights = jnp.exp2(scores * SCALE - best).astype(BF16)
    part = jnp.dot(weights, values, preferred_element_type=F32)
    if top is None:
        return best, part
    return best, mixed * jnp.exp2(top - best) + part


def load_state(top, mixed):
    total = jnp.broadcast_to(top[:, HD // 2 : HD // 2 + 1], mixed.shape)
    return top[:, :1], jnp.concatenate([mixed, total], axis=1)


def store_state(best, mixed):
    low = lax.broadcasted_iota(jnp.int32, mixed[:, :HD].shape, 1) < HD // 2
    return jnp.where(low, best, mixed[:, HD:]), mixed[:, :HD]


def stage(blocks, keys, values, start):
    for block in blocks:
        for j in range(block.shape[0]):
            keys[start : start + PIECE] = block[j, 0]
            values[start : start + PIECE, :HD] = block[j, 1]
            start += PIECE
    return start


def head(query, r, h):
    return query[r : r + TILE, h * HD : (h + 1) * HD]


def attend_first(count, query, own, *refs):
    blocks, (top_out, mixed_out, token, keys, values) = refs[:count], refs[count:]
    token[...] = jnp.zeros_like(token)
    prompt = stage(blocks, keys, values, 0)
    keys[prompt:] = own[0]
    values[prompt:, :HD] = own[1]
    values[:, HD:] = jnp.ones((values.shape[0], HD), BF16)

    for h in range(GROUPS):
        for r in range(0, CLEN, TILE):
            lines = head(query, r, h)
            extent = prompt + r + TILE
            column = lax.broadcasted_iota(jnp.int32, (TILE, extent), 1)
            row = lax.broadcasted_iota(jnp.int32, (TILE, extent), 0)
            best, mixed = absorb(
                lines, keys[:extent], values[:extent], None, None, column - row <= extent - TILE
            )
            top_out[h, r : r + TILE], mixed_out[h, r : r + TILE] = store_state(best, mixed)


def attend_more(count, width, query, *refs):
    blocks, (top_in, mixed_in, top_out, mixed_out, token, keys, values) = (
        refs[:count],
        refs[count:],
    )
    token[...] = jnp.zeros_like(token)
    stage(blocks, keys, values, 0)
    values[:, HD:] = jnp.ones((values.shape[0], HD), BF16)

    for h in range(GROUPS):
        for r in range(0, CLEN, TILE):
            best, mixed = load_state(top_in[h, r : r + TILE], mixed_in[h, r : r + TILE])
            for at in range(0, keys.shape[0], width):
                best, mixed = absorb(
                    head(query, r, h), keys[at : at + width], values[at : at + width], best, mixed
                )
            top_out[h, r : r + TILE], mixed_out[h, r : r + TILE] = store_state(best, mixed)


def attend_last(count, place, query, *refs):
    blocks, (top_in, mixed_in, o0, o1, o2, o3, context, keys, values) = (
        refs[:count],
        refs[count:],
    )
    x, live = place[0], place[3]
    stage(blocks, keys, values, 0)
    values[:, HD:] = jnp.ones((values.shape[0], HD), BF16)

    for h in range(GROUPS):
        for r in range(0, CLEN, TILE):
            best, mixed = load_state(top_in[h, r : r + TILE], mixed_in[h, r : r + TILE])
            best, mixed = absorb(head(query, r, h), keys[...], values[...], best, mixed)
            line = lax.broadcasted_iota(jnp.int32, (TILE, HD), 0) + r
            context[r : r + TILE, h * HD : (h + 1) * HD] = jnp.where(
                line < live, mixed[:, :HD] / mixed[:, HD:], 0.0
            ).astype(BF16)
    for d, out in enumerate((o0, o1, o2, o3)):
        out[...] = context[pl.ds(pl.multiple_of(lax.rem(x + d, 4) * 128, 128), 128)]


def cost(rows, keys):
    return pl.CostEstimate(
        flops=24 * rows * keys * HD, bytes_accessed=12 << 20, transcendentals=0
    )


STATE = [jax.ShapeDtypeStruct((GROUPS, CLEN, HD), F32)] * 2
TOKEN = jax.ShapeDtypeStruct((8, HD), F32)


def room(blocks, more=0):
    extent = sum(b.shape[0] for b in blocks) * PIECE + more
    return [pltpu.VMEM((extent, HD), BF16), pltpu.VMEM((extent, 2 * HD), BF16)]


def first_part(query, own, blocks):
    return pl.pallas_call(
        functools.partial(attend_first, len(blocks)),
        in_specs=[VMEM] * (2 + len(blocks)),
        out_specs=[VMEM] * 3,
        out_shape=STATE + [TOKEN],
        scratch_shapes=room(blocks, CLEN),
        compiler_params=PARAMS,
        cost_estimate=cost(GROUPS * CLEN, 2048),
    )(query, own, *blocks)


def more_part(query, blocks, state, width, leave=False):
    return pl.pallas_call(
        functools.partial(attend_more, len(blocks), width),
        in_specs=[VMEM] * (3 + len(blocks)),
        out_specs=[VMEM] * 3,
        out_shape=([pltpu.HBM(s.shape, s.dtype) for s in STATE] if leave else STATE) + [TOKEN],
        scratch_shapes=room(blocks),
        compiler_params=PARAMS,
        cost_estimate=cost(GROUPS * CLEN, 1024),
    )(query, *blocks, *state)


def last_part(place, query, blocks, state):
    return pl.pallas_call(
        functools.partial(attend_last, len(blocks)),
        in_specs=[SMEM] + [VMEM] * (3 + len(blocks)),
        out_specs=[VMEM] * 4,
        out_shape=[jax.ShapeDtypeStruct((128, GROUPS * HD), BF16)] * 4,
        scratch_shapes=[pltpu.VMEM((CLEN, GROUPS * HD), BF16)] + room(blocks),
        compiler_params=PARAMS,
        cost_estimate=cost(GROUPS * CLEN, 1024),
    )(place, query, *blocks, *state)


def whole(a):
    return pl.BlockSpec(a.shape, lambda h: (0,) * a.ndim)


def gate(value, *refs):
    refs[-1][...] = value[...]


def gated(value, ready):
    return pl.pallas_call(
        gate,
        in_specs=[VMEM, ANY],
        out_specs=VMEM,
        out_shape=jax.ShapeDtypeStruct(value.shape, value.dtype),
        compiler_params=PARAMS,
    )(value, ready)


def widen(b0, b1, b2, b3, *refs):
    out = refs[-1]
    for j, block in enumerate((b0, b1, b2, b3)):
        out[:, j * 640 : (j + 1) * 640] = block[...]


def widened(blocks, *ready):
    return pl.pallas_call(
        widen,
        in_specs=[VMEM] * 4 + [ANY] * len(ready),
        out_specs=VMEM,
        out_shape=jax.ShapeDtypeStruct((80, 2560), BF16),
        compiler_params=PARAMS,
    )(*blocks, *ready)


def pack(place, *refs):
    blocks, out = refs[:-1], refs[-1]
    out[0] = blocks[0][...]
    for i in range(1, 4):
        out[i] = blocks[i][...]
    if len(blocks) > 4:

        @pl.when(place[2] == 1)
        def _():
            for i in range(1, 4):
                out[i] = blocks[i + 3][...]


def packed(place, *blocks):
    return pl.pallas_call(
        pack,
        in_specs=[SMEM] + [VMEM] * len(blocks),
        out_specs=VMEM,
        out_shape=jax.ShapeDtypeStruct((4, *blocks[0].shape), BF16),
        compiler_params=PARAMS,
    )(place, *blocks)


def project(place, c0, c1, c2, c3, columns, o0, o1, o2, o3, lines):
    contexts, outs = (c0, c1, c2, c3), (o0, o1, o2, o3)
    rows, depth = c0.shape[1:]

    def lay(pick):
        for d in range(4):
            for j in range(4):
                lines[d * rows : (d + 1) * rows, j * depth : (j + 1) * depth] = pick(d, j)

    @pl.when((pl.program_id(0) == 0) & (place[2] == 0))
    def _():
        lay(lambda d, j: contexts[j][(d - j) % 4])

    @pl.when((pl.program_id(0) == 0) & (place[2] == 1))
    def _():
        lay(lambda d, j: contexts[d][j])

    total = lax.dot_general(lines[...], columns[...], NT, preferred_element_type=F32)
    total = total.astype(BF16)
    for d, out in enumerate(outs):
        out[...] = total[d * rows : (d + 1) * rows]


def projected(place, contexts, columns):
    rows = contexts[0].shape[1]
    block = jax.ShapeDtypeStruct((rows, 1280), BF16)
    return pl.pallas_call(
        project,
        grid=(5,),
        in_specs=[SMEM]
        + [whole(c) for c in contexts]
        + [pl.BlockSpec((256, 2560), lambda n: (n, 0))],
        out_specs=[pl.BlockSpec((rows, 256), lambda n: (0, n))] * 4,
        out_shape=[block] * 4,
        scratch_shapes=[pltpu.VMEM((4 * rows, 2560), BF16)],
        compiler_params=pltpu.CompilerParams(vmem_limit_bytes=24 << 20),
        cost_estimate=pl.CostEstimate(
            flops=2 * 4 * rows * 2560 * 1280, bytes_accessed=10 << 20, transcendentals=0
        ),
    )(place, *contexts, columns)


def finish(place, p0, p1, p2, p3, residual, gain, attended, normed):
    quarter = place[0] + place[1]
    for d, part in enumerate((p0, p1, p2, p3)):
        at = pl.multiple_of(lax.rem(quarter + d, 4) * 1280, 1280)
        attended[:, pl.ds(at, 1280)] = part[...]
    for r in range(0, residual.shape[0], 16):
        stream = residual[r : r + 16].astype(F32) + attended[r : r + 16].astype(F32)
        power = jnp.mean(stream * stream, axis=-1, keepdims=True)
        normed[r : r + 16] = (stream * lax.rsqrt(power + 1e-06) * gain[...]).astype(BF16)


def finished(place, parts, residual, gain):
    block = jax.ShapeDtypeStruct((128, 5120), BF16)
    lines = 64
    wide = pl.BlockSpec((lines, 5120), lambda n: (n, 0))
    return pl.pallas_call(
        finish,
        grid=(128 // lines,),
        in_specs=[SMEM]
        + [pl.BlockSpec((lines, 1280), lambda n: (n, 0))] * 4
        + [wide, pl.BlockSpec((1, 5120), lambda n: (0, 0))],
        out_specs=[wide] * 2,
        out_shape=[block] * 2,
        compiler_params=PARAMS,
    )(place, *parts, residual, gain)


SWAP = [(i, i ^ 1) for i in range(16)]


def along(distance):
    return [
        (g, (g // 2 + (distance if g % 2 == 0 else -distance)) % 8 * 2 + g % 2) for g in range(16)
    ]


EVERY = ("dp", "group", "tensor")


def ring(step):
    pairs = []
    for y in range(4):
        for g in range(16):
            for x in range(4):
                to = (y, (x + step) % 4) if g % 2 == 0 else ((y + step) % 4, x)
                pairs.append(((y * 16 + g) * 4 + x, (to[0] * 16 + g) * 4 + to[1]))
    return pairs


SLANT = [(y * 4 + x, (y - x) % 4 * 4 + x) for y in range(4) for x in range(4)]


def around(axes, ways, behind, across, ahead):
    return [
        lax.ppermute(a, axes, way)
        for a, way in zip((behind, across, ahead), (ways(-1), ways(2), ways(1)))
    ]


def plain(step):
    return [(i, (i + step) % 4) for i in range(4)]


def kept(arrays):
    return [pltpu.with_memory_space_constraint(a, pltpu.HBM) for a in arrays]


def shards(queries, comp_kv, prompt_kv, residual, out_weight, gain, lengths):
    x, y, group = lax.axis_index("tensor"), lax.axis_index("dp"), lax.axis_index("group")
    place = jnp.stack([x, y, group % 2, lengths[0, 0]]).astype(jnp.int32)
    query = queries[0, 0]
    swap = functools.partial(lax.ppermute, axis_name="group", perm=SWAP)

    with jax.named_scope("prompt"):
        piece = prompt_kv[0].transpose(1, 0, 2)[None]
        pair = jnp.concatenate([piece, swap(piece)], axis=0)

    weight = out_weight.T
    own = comp_kv[0, 0].transpose(1, 0, 2)
    with jax.named_scope("weights"):
        pieces = around("tensor", plain, weight, weight, weight)
    with jax.named_scope("attention"):
        z1 = lax.ppermute(pair, "group", along(1))
        *state, token = first_part(query, own, [pair])
    with jax.named_scope("weights"):
        wide = widened([weight, *pieces], token)
        pieces = lax.ppermute(wide, ("dp", "tensor"), SLANT)
    with jax.named_scope("attention"):
        z1 = gated(z1, wide)
        z2 = lax.ppermute(z1, "group", along(1))
        z4 = lax.ppermute(z1[:1], "group", along(3))
        *state, token = more_part(query, [z1, swap(z1)], state, 1024, True)
        z2 = gated(z2, token)
        z4 = gated(z4, z2)
    with jax.named_scope("weights"):
        columns = lax.all_gather(gated(pieces, z4), "group", axis=0, tiled=True)
    with jax.named_scope("attention"):
        z3 = lax.ppermute(z2, "group", along(1))
        *state, token = more_part(
            query, [z2, z4, swap(z2), swap(z4)], kept(state), 1536, True
        )
        z3 = gated(z3, token)
        c0, c1, c2, c3 = last_part(place, query, [z3, swap(z3)], kept(state))

    with jax.named_scope("exchange"):
        blocks = around("tensor", plain, c3, c2, c1)
        mixed = packed(place, c0, c1, c2, c3, *blocks)
        contexts = [mixed] + around(EVERY, ring, mixed, mixed, mixed)

    with jax.named_scope("project"):
        o0, o1, o2, o3 = projected(place, kept(contexts), *kept([columns]))
        parts = [o0] + around(EVERY, ring, o3, o2, o1)
    with jax.named_scope("finish"):
        attended, normed = finished(place, parts, residual[0, 0], gain[None])
    return (attended[None, None], normed[None, None])


def solution(mesh):
    in_specs = (
        P("dp", "group", None, "tensor"),
        P("dp", "group", None, None, "tensor"),
        P("dp", "group", None, "tensor"),
        P("dp", "group", "tensor", None),
        P("tensor", ("dp", "group")),
        P(),
        P("dp", "group"),
    )
    out_specs = (P("dp", "group", "tensor", None), P("dp", "group", "tensor", None))
    return jax.shard_map(shards, mesh=mesh, in_specs=in_specs, out_specs=out_specs, check_vma=False)
```

```python
import functools

import jax
import jax.numpy as jnp
import numpy as np
from jax import lax
from jax.experimental import pallas as pl
from jax.experimental.pallas import tpu as pltpu
from jax.sharding import PartitionSpec as P

HD = 128
GROUPS = 5
CLEN = 512
PIECE = 256
SCALE = float(HD**-0.5 * np.log2(np.e))
F32 = jnp.float32
BF16 = jnp.bfloat16
NT = (((1,), (1,)), ((), ()))
ANY = pl.BlockSpec(memory_space=pl.ANY)
SMEM = pl.BlockSpec(memory_space=pltpu.SMEM)
VMEM = pl.BlockSpec(memory_space=pltpu.VMEM)
TILE = 256
PARAMS = pltpu.CompilerParams(vmem_limit_bytes=20 << 20)


def absorb(rows, keys, values, top, mixed, mask=None):
    scores = lax.dot_general(rows, keys, NT, preferred_element_type=F32)
    if mask is not None:
        scores = jnp.where(mask, scores, jnp.float32(-1e30))
    best = jnp.max(scores, axis=-1, keepdims=True) * SCALE
    if top is not None:
        best = jnp.maximum(top, best)
    weights = jnp.exp2(scores * SCALE - best).astype(BF16)
    part = jnp.dot(weights, values, preferred_element_type=F32)
    if top is None:
        return best, part
    return best, mixed * jnp.exp2(top - best) + part


def load_state(top, mixed):
    total = jnp.broadcast_to(top[:, HD // 2 : HD // 2 + 1], mixed.shape)
    return top[:, :1], jnp.concatenate([mixed, total], axis=1)


def store_state(best, mixed):
    low = lax.broadcasted_iota(jnp.int32, mixed[:, :HD].shape, 1) < HD // 2
    return jnp.where(low, best, mixed[:, HD:]), mixed[:, :HD]


def stage(blocks, keys, values, start):
    for block in blocks:
        for j in range(block.shape[0]):
            keys[start : start + PIECE] = block[j, 0]
            values[start : start + PIECE, :HD] = block[j, 1]
            start += PIECE
    return start


def head(query, r, h):
    return query[r : r + TILE, h * HD : (h + 1) * HD]


def attend_first(count, query, own, *refs):
    blocks, (top_out, mixed_out, token, keys, values) = refs[:count], refs[count:]
    token[...] = jnp.zeros_like(token)
    prompt = stage(blocks, keys, values, 0)
    keys[prompt:] = own[0]
    values[prompt:, :HD] = own[1]
    values[:, HD:] = jnp.ones((values.shape[0], HD), BF16)

    for h in range(GROUPS):
        for r in range(0, CLEN, TILE):
            lines = head(query, r, h)
            extent = prompt + r + TILE
            column = lax.broadcasted_iota(jnp.int32, (TILE, extent), 1)
            row = lax.broadcasted_iota(jnp.int32, (TILE, extent), 0)
            best, mixed = absorb(
                lines, keys[:extent], values[:extent], None, None, column - row <= extent - TILE
            )
            top_out[h, r : r + TILE], mixed_out[h, r : r + TILE] = store_state(best, mixed)


def attend_more(count, width, query, *refs):
    blocks, (top_in, mixed_in, top_out, mixed_out, token, keys, values) = (
        refs[:count],
        refs[count:],
    )
    token[...] = jnp.zeros_like(token)
    stage(blocks, keys, values, 0)
    values[:, HD:] = jnp.ones((values.shape[0], HD), BF16)

    for h in range(GROUPS):
        for r in range(0, CLEN, TILE):
            best, mixed = load_state(top_in[h, r : r + TILE], mixed_in[h, r : r + TILE])
            for at in range(0, keys.shape[0], width):
                best, mixed = absorb(
                    head(query, r, h), keys[at : at + width], values[at : at + width], best, mixed
                )
            top_out[h, r : r + TILE], mixed_out[h, r : r + TILE] = store_state(best, mixed)


def attend_last(count, place, query, *refs):
    blocks, (top_in, mixed_in, o0, o1, o2, o3, context, keys, values) = (
        refs[:count],
        refs[count:],
    )
    x, live = place[0], place[3]
    stage(blocks, keys, values, 0)
    values[:, HD:] = jnp.ones((values.shape[0], HD), BF16)

    for h in range(GROUPS):
        for r in range(0, CLEN, TILE):
            best, mixed = load_state(top_in[h, r : r + TILE], mixed_in[h, r : r + TILE])
            best, mixed = absorb(head(query, r, h), keys[...], values[...], best, mixed)
            line = lax.broadcasted_iota(jnp.int32, (TILE, HD), 0) + r
            context[r : r + TILE, h * HD : (h + 1) * HD] = jnp.where(
                line < live, mixed[:, :HD] / mixed[:, HD:], 0.0
            ).astype(BF16)
    for d, out in enumerate((o0, o1, o2, o3)):
        out[...] = context[pl.ds(pl.multiple_of(lax.rem(x + d, 4) * 128, 128), 128)]


def cost(rows, keys):
    return pl.CostEstimate(
        flops=24 * rows * keys * HD, bytes_accessed=12 << 20, transcendentals=0
    )


STATE = [jax.ShapeDtypeStruct((GROUPS, CLEN, HD), F32)] * 2
TOKEN = jax.ShapeDtypeStruct((8, HD), F32)


def room(blocks, more=0):
    extent = sum(b.shape[0] for b in blocks) * PIECE + more
    return [pltpu.VMEM((extent, HD), BF16), pltpu.VMEM((extent, 2 * HD), BF16)]


def first_part(query, own, blocks):
    return pl.pallas_call(
        functools.partial(attend_first, len(blocks)),
        in_specs=[VMEM] * (2 + len(blocks)),
        out_specs=[VMEM] * 3,
        out_shape=STATE + [TOKEN],
        scratch_shapes=room(blocks, CLEN),
        compiler_params=PARAMS,
        cost_estimate=cost(GROUPS * CLEN, 2048),
    )(query, own, *blocks)


def more_part(query, blocks, state, width, leave=False):
    return pl.pallas_call(
        functools.partial(attend_more, len(blocks), width),
        in_specs=[VMEM] * (3 + len(blocks)),
        out_specs=[VMEM] * 3,
        out_shape=([pltpu.HBM(s.shape, s.dtype) for s in STATE] if leave else STATE) + [TOKEN],
        scratch_shapes=room(blocks),
        compiler_params=PARAMS,
        cost_estimate=cost(GROUPS * CLEN, 1024),
    )(query, *blocks, *state)


def last_part(place, query, blocks, state):
    return pl.pallas_call(
        functools.partial(attend_last, len(blocks)),
        in_specs=[SMEM] + [VMEM] * (3 + len(blocks)),
        out_specs=[VMEM] * 4,
        out_shape=[jax.ShapeDtypeStruct((128, GROUPS * HD), BF16)] * 4,
        scratch_shapes=[pltpu.VMEM((CLEN, GROUPS * HD), BF16)] + room(blocks),
        compiler_params=PARAMS,
        cost_estimate=cost(GROUPS * CLEN, 1024),
    )(place, query, *blocks, *state)


def whole(a):
    return pl.BlockSpec(a.shape, lambda h: (0,) * a.ndim)


def gate(value, *refs):
    refs[-1][...] = value[...]


def gated(value, ready):
    return pl.pallas_call(
        gate,
        in_specs=[VMEM, ANY],
        out_specs=VMEM,
        out_shape=jax.ShapeDtypeStruct(value.shape, value.dtype),
        compiler_params=PARAMS,
    )(value, ready)


def widen(b0, b1, b2, b3, *refs):
    out = refs[-1]
    for j, block in enumerate((b0, b1, b2, b3)):
        out[:, j * 640 : (j + 1) * 640] = block[...]


def widened(blocks, *ready):
    return pl.pallas_call(
        widen,
        in_specs=[VMEM] * 4 + [ANY] * len(ready),
        out_specs=VMEM,
        out_shape=jax.ShapeDtypeStruct((80, 2560), BF16),
        compiler_params=PARAMS,
    )(*blocks, *ready)


def pack(place, *refs):
    blocks, out = refs[:-1], refs[-1]
    out[0] = blocks[0][...]
    for i in range(1, 4):
        out[i] = blocks[i][...]
    if len(blocks) > 4:

        @pl.when(place[2] == 1)
        def _():
            for i in range(1, 4):
                out[i] = blocks[i + 3][...]


def packed(place, *blocks):
    return pl.pallas_call(
        pack,
        in_specs=[SMEM] + [VMEM] * len(blocks),
        out_specs=VMEM,
        out_shape=jax.ShapeDtypeStruct((4, *blocks[0].shape), BF16),
        compiler_params=PARAMS,
    )(place, *blocks)


def project(place, c0, c1, c2, c3, columns, o0, o1, o2, o3, lines):
    contexts, outs = (c0, c1, c2, c3), (o0, o1, o2, o3)
    rows, depth = c0.shape[1:]

    def lay(pick):
        for d in range(4):
            for j in range(4):
                lines[d * rows : (d + 1) * rows, j * depth : (j + 1) * depth] = pick(d, j)

    @pl.when((pl.program_id(0) == 0) & (place[2] == 0))
    def _():
        lay(lambda d, j: contexts[j][(d - j) % 4])

    @pl.when((pl.program_id(0) == 0) & (place[2] == 1))
    def _():
        lay(lambda d, j: contexts[d][j])

    total = lax.dot_general(lines[...], columns[...], NT, preferred_element_type=F32)
    total = total.astype(BF16)
    for d, out in enumerate(outs):
        out[...] = total[d * rows : (d + 1) * rows]


def projected(place, contexts, columns):
    rows = contexts[0].shape[1]
    block = jax.ShapeDtypeStruct((rows, 1280), BF16)
    return pl.pallas_call(
        project,
        grid=(5,),
        in_specs=[SMEM]
        + [whole(c) for c in contexts]
        + [pl.BlockSpec((256, 2560), lambda n: (n, 0))],
        out_specs=[pl.BlockSpec((rows, 256), lambda n: (0, n))] * 4,
        out_shape=[block] * 4,
        scratch_shapes=[pltpu.VMEM((4 * rows, 2560), BF16)],
        compiler_params=pltpu.CompilerParams(vmem_limit_bytes=24 << 20),
        cost_estimate=pl.CostEstimate(
            flops=2 * 4 * rows * 2560 * 1280, bytes_accessed=10 << 20, transcendentals=0
        ),
    )(place, *contexts, columns)


def finish(place, p0, p1, p2, p3, residual, gain, attended, normed):
    quarter = place[0] + place[1]
    for d, part in enumerate((p0, p1, p2, p3)):
        at = pl.multiple_of(lax.rem(quarter + d, 4) * 1280, 1280)
        attended[:, pl.ds(at, 1280)] = part[...]
    for r in range(0, residual.shape[0], 16):
        stream = residual[r : r + 16].astype(F32) + attended[r : r + 16].astype(F32)
        power = jnp.mean(stream * stream, axis=-1, keepdims=True)
        normed[r : r + 16] = (stream * lax.rsqrt(power + 1e-06) * gain[...]).astype(BF16)


def finished(place, parts, residual, gain):
    block = jax.ShapeDtypeStruct((128, 5120), BF16)
    lines = 64
    wide = pl.BlockSpec((lines, 5120), lambda n: (n, 0))
    return pl.pallas_call(
        finish,
        grid=(128 // lines,),
        in_specs=[SMEM]
        + [pl.BlockSpec((lines, 1280), lambda n: (n, 0))] * 4
        + [wide, pl.BlockSpec((1, 5120), lambda n: (0, 0))],
        out_specs=[wide] * 2,
        out_shape=[block] * 2,
        compiler_params=PARAMS,
    )(place, *parts, residual, gain)


SWAP = [(i, i ^ 1) for i in range(16)]


def along(distance):
    return [
        (g, (g // 2 + (distance if g % 2 == 0 else -distance)) % 8 * 2 + g % 2) for g in range(16)
    ]


EVERY = ("dp", "group", "tensor")


def ring(step):
    pairs = []
    for y in range(4):
        for g in range(16):
            for x in range(4):
                to = (y, (x + step) % 4) if g % 2 == 0 else ((y + step) % 4, x)
                pairs.append(((y * 16 + g) * 4 + x, (to[0] * 16 + g) * 4 + to[1]))
    return pairs


SLANT = [(y * 4 + x, (y - x) % 4 * 4 + x) for y in range(4) for x in range(4)]


def around(axes, ways, behind, across, ahead):
    return [
        lax.ppermute(a, axes, way)
        for a, way in zip((behind, across, ahead), (ways(-1), ways(2), ways(1)))
    ]


def plain(step):
    return [(i, (i + step) % 4) for i in range(4)]


def kept(arrays):
    return [pltpu.with_memory_space_constraint(a, pltpu.HBM) for a in arrays]


def shards(queries, comp_kv, prompt_kv, residual, out_weight, gain, lengths):
    x, y, group = lax.axis_index("tensor"), lax.axis_index("dp"), lax.axis_index("group")
    place = jnp.stack([x, y, group % 2, lengths[0, 0]]).astype(jnp.int32)
    query = queries[0, 0]
    swap = functools.partial(lax.ppermute, axis_name="group", perm=SWAP)

    with jax.named_scope("prompt"):
        piece = prompt_kv[0].transpose(1, 0, 2)[None]
        pair = jnp.concatenate([piece, swap(piece)], axis=0)

    weight = out_weight.T
    own = comp_kv[0, 0].transpose(1, 0, 2)
    with jax.named_scope("weights"):
        pieces = around("tensor", plain, weight, weight, weight)
    with jax.named_scope("attention"):
        z1 = lax.ppermute(pair, "group", along(1))
        *state, token = first_part(query, own, [pair])
    with jax.named_scope("weights"):
        wide = widened([weight, *pieces], token)
        pieces = lax.ppermute(wide, ("dp", "tensor"), SLANT)
    with jax.named_scope("attention"):
        z1 = gated(z1, wide)
        z2 = lax.ppermute(z1, "group", along(1))
        z4 = lax.ppermute(z1[:1], "group", along(3))
        *state, token = more_part(query, [z1, swap(z1)], state, 1024, True)
        z2 = gated(z2, token)
        z4 = gated(z4, z2)
    with jax.named_scope("weights"):
        columns = lax.all_gather(gated(pieces, z4), "group", axis=0, tiled=True)
    with jax.named_scope("attention"):
        z3 = lax.ppermute(z2, "group", along(1))
        *state, token = more_part(
            query, [z2, z4, swap(z2), swap(z4)], kept(state), 768, True
        )
        z3 = gated(z3, token)
        c0, c1, c2, c3 = last_part(place, query, [z3, swap(z3)], kept(state))

    with jax.named_scope("exchange"):
        blocks = around("tensor", plain, c3, c2, c1)
        mixed = packed(place, c0, c1, c2, c3, *blocks)
        contexts = [mixed] + around(EVERY, ring, mixed, mixed, mixed)

    with jax.named_scope("project"):
        o0, o1, o2, o3 = projected(place, kept(contexts), *kept([columns]))
        parts = [o0] + around(EVERY, ring, o3, o2, o1)
    with jax.named_scope("finish"):
        attended, normed = finished(place, parts, residual[0, 0], gain[None])
    return (attended[None, None], normed[None, None])


def solution(mesh):
    in_specs = (
        P("dp", "group", None, "tensor"),
        P("dp", "group", None, None, "tensor"),
        P("dp", "group", None, "tensor"),
        P("dp", "group", "tensor", None),
        P("tensor", ("dp", "group")),
        P(),
        P("dp", "group"),
    )
    out_specs = (P("dp", "group", "tensor", None), P("dp", "group", "tensor", None))
    return jax.shard_map(shards, mesh=mesh, in_specs=in_specs, out_specs=out_specs, check_vma=False)
```
